32 devices in a mesh: grp: 2 (over y), row: 4 (over x, core), col: 4 (over z).
Axes of the slice: x: 2, y: 2, z: 4, core: 2. Of those that a mesh axis runs over, the one named last changes fastest.
Arguments:
- gen_coords: bfloat16 [3, 192, 24576], P(None, None, ('grp', 'row', 'col')), parts along dimension 2, may hold values from -30 to 30
- ref_coords: bfloat16 [3, 192, 24576], P(None, None, ('grp', 'row', 'col')), parts along dimension 2, may hold values from -30 to 30
- threshold: float32 [1], replicated, may hold values from 0.75 to 2
Outputs:
- gen_best: float32 [24576], P(('grp', 'row', 'col')), parts along dimension 0
- ref_best: float32 [24576], P(('grp', 'row', 'col')), parts along dimension 0
- ref_cover: float32 [24576], P(('grp', 'row', 'col')), parts along dimension 0
The draws below stay inside these ranges and needn't reach their ends.
There are 2 independent parts, one for each index of `grp`. The reference program is written for one: setup_inputs(seed, part) draws one part's arguments, and reference() takes and returns one part's arrays. A program takes and returns all parts, laid end to end along the dimension named above; an argument that names none is the same for every part. Nothing has to cross between parts.
All inputs are finite; a program needn't handle non-finite values.
Results may differ from the reference program's by a relative error of at most 0.0003.
Values may be sent and summed in bfloat16 or wider, within the bound.
A program may use at most 64 MiB of HBM per device.

```python
import math
import jax
import jax.numpy as jnp
from jax import lax

ATOMS = 192
FRAMES = 768
POLAR = 8
STEPS = 2
GRID_ROWS = 4
GRID_COLS = 4
GEN_FRAMES = 12288
REF_FRAMES = 12288


def cycle_base(key):
    keys = jax.random.split(key, 3)
    angle = 2.0 * math.pi * jnp.arange(ATOMS, dtype=jnp.float32) / ATOMS + jax.random.uniform(keys[0], (ATOMS,), jnp.float32, -0.01, 0.01)
    radius = 6.0 + jax.random.uniform(keys[1], (ATOMS,), jnp.float32, -1.5, 1.5)
    height = 1.5 * jnp.sin(3.0 * angle) + 0.8 * jax.random.truncated_normal(keys[2], -3.0, 3.0, (ATOMS,), jnp.float32)
    return jnp.stack([radius * jnp.cos(angle), radius * jnp.sin(angle), height])


def place(key, base, noise, lowest, highest):
    frames = noise.shape[2]
    keys = jax.random.split(key, 4)
    spread = jnp.exp(jax.random.uniform(keys[0], (frames,), jnp.float32, math.log(lowest), math.log(highest)))
    points = base[:, :, None] + noise * spread
    first = jax.random.uniform(keys[1], (frames,), jnp.float32, -math.pi, math.pi)
    second = jax.random.uniform(keys[2], (frames,), jnp.float32, -math.pi, math.pi)
    cos_one = jnp.cos(first)
    sin_one = jnp.sin(first)
    cos_two = jnp.cos(second)
    sin_two = jnp.sin(second)
    turned_x = cos_one * points[0] - sin_one * points[1]
    turned_y = sin_one * points[0] + cos_one * points[1]
    final_y = cos_two * turned_y - sin_two * points[2]
    final_z = sin_two * turned_y + cos_two * points[2]
    offset = jax.random.uniform(keys[3], (3, frames), jnp.float32, -8.0, 8.0)
    placed = jnp.stack([turned_x, final_y, final_z]) + offset[:, None, :]
    return placed.astype(jnp.bfloat16)


def draw_gen_coords(key, part):
    base = cycle_base(key)
    key = jax.random.fold_in(key, 11)
    noise_key, place_key = jax.random.split(key)
    noise = jax.random.truncated_normal(noise_key, -4.0, 4.0, (3, ATOMS, GEN_FRAMES), jnp.float32)
    return place(place_key, base, noise, 0.15, 1.2)


def draw_ref_coords(key, part):
    base = cycle_base(key)
    key = jax.random.fold_in(key, 23)
    noise_key, place_key = jax.random.split(key)
    noise = jax.random.truncated_normal(noise_key, -4.0, 4.0, (3, ATOMS, REF_FRAMES), jnp.float32)
    return place(place_key, base, noise, 0.15, 1.2)


def setup_inputs(seed: int = 0, part: int = 0) -> dict:
    streams_of = jax.random.split(jax.random.key(seed), 4)
    part_keys = jax.random.split(jax.random.fold_in(streams_of[3], part), 4)
    gen_coords = draw_gen_coords(jax.random.fold_in(jax.random.fold_in(streams_of[3], part), 71), part)
    ref_coords = draw_ref_coords(jax.random.fold_in(jax.random.fold_in(streams_of[3], part), 71), part)
    threshold = jnp.clip(jax.random.uniform(streams_of[2], (1,), jnp.float32, 0.75, 2.0), 0.75, 2.0)
    return dict(gen_coords=gen_coords, ref_coords=ref_coords, threshold=threshold)


soft_width = 0.25
floor_term = 0.01

def centered(coords):
    points = coords.astype(jnp.float32)
    middle = lax.optimization_barrier(jnp.mean(points, axis=1, keepdims=True))
    return points - middle

def squares(frames_c):
    return lax.optimization_barrier(jnp.sum(frames_c * frames_c, axis=(0, 1)))

def newton_trace(entries):
    squared = entries[0] * entries[0]
    for entry in entries[1:]:
        squared = squared + entry * entry
    inverse = lax.rsqrt(squared + 1.0)
    factor = [entry * inverse for entry in entries]
    for sweep in range(POLAR):
        gram = [[factor[source] * factor[target] + factor[3 + source] * factor[3 + target] + factor[6 + source] * factor[6 + target] for target in range(3)] for source in range(3)]
        factor = [1.5 * factor[3 * source + target] - 0.5 * (factor[3 * source] * gram[0][target] + factor[3 * source + 1] * gram[1][target] + factor[3 * source + 2] * gram[2][target]) for source in range(3) for target in range(3)]
    result = factor[0] * entries[0]
    for position in range(1, 9):
        result = result + factor[position] * entries[position]
    return result

def tile_stats(gen_c, ref_c, threshold):
    gen_sq = squares(gen_c)
    ref_sq = squares(ref_c)
    frames = gen_c.shape[2]
    block_width = min(128, frames)
    block_count = frames // block_width

    def visit(running, block_index):
        ref_low, ref_hits = running
        piece = lax.dynamic_slice_in_dim(gen_c, block_index * block_width, block_width, 2)
        piece_sq = lax.dynamic_slice_in_dim(gen_sq, block_index * block_width, block_width, 0)
        covariance = jnp.einsum('aif,bie->afbe', piece, ref_c, precision=lax.Precision.HIGHEST)
        entries = [covariance[source, :, target, :] for source in range(3) for target in range(3)]
        align = newton_trace(entries)
        rmsd = jnp.sqrt((piece_sq[:, None] + ref_sq[None, :] - 2.0 * align) / ATOMS + floor_term)
        weights = jax.nn.sigmoid((threshold - rmsd) / soft_width)
        return ((jnp.minimum(ref_low, lax.optimization_barrier(jnp.min(rmsd, axis=0))), ref_hits + lax.optimization_barrier(jnp.sum(weights, axis=0))), lax.optimization_barrier(jnp.min(rmsd, axis=1)))
    start = (jnp.full((frames,), jnp.inf, jnp.float32), jnp.zeros((frames,), jnp.float32))
    (ref_low, ref_hits), gen_low = lax.scan(visit, start, jnp.arange(block_count, dtype=jnp.int32))
    return (gen_low.reshape(frames), ref_low, ref_hits)

def reference(gen_coords, ref_coords, threshold):
    limit = threshold[0]
    gen_grid = gen_coords.reshape(3, ATOMS, GRID_ROWS, GRID_COLS, FRAMES)
    ref_grid = ref_coords.reshape(3, ATOMS, GRID_ROWS, GRID_COLS, FRAMES)
    gen_out = None
    ref_out = None
    cover_out = None
    for step_index in range(STEPS):
        row_move = step_index + step_index // GRID_COLS

        def visit_cell(cell):
            grid_row = cell // GRID_COLS
            grid_col = cell % GRID_COLS
            gen_col = (grid_col - grid_row - step_index) % GRID_COLS
            ref_row = (grid_row - row_move) % GRID_ROWS
            gen_block = lax.dynamic_index_in_dim(lax.dynamic_index_in_dim(gen_grid, grid_row, 2, False), gen_col, 2, False)
            ref_block = lax.dynamic_index_in_dim(lax.dynamic_index_in_dim(ref_grid, ref_row, 2, False), grid_col, 2, False)
            return tile_stats(centered(gen_block), centered(ref_block), limit)
        gen_low, ref_low, ref_hits = lax.map(visit_cell, jnp.arange(GRID_ROWS * GRID_COLS, dtype=jnp.int32))
        home_cols = (jnp.arange(GRID_COLS, dtype=jnp.int32)[None, :] + jnp.arange(GRID_ROWS, dtype=jnp.int32)[:, None] + step_index) % GRID_COLS
        gen_low = jnp.take_along_axis(gen_low.reshape(GRID_ROWS, GRID_COLS, FRAMES), home_cols[:, :, None], axis=1)
        ref_low = jnp.roll(ref_low.reshape(GRID_ROWS, GRID_COLS, FRAMES), -row_move, axis=0)
        ref_hits = jnp.roll(ref_hits.reshape(GRID_ROWS, GRID_COLS, FRAMES), -row_move, axis=0)
        if step_index == 0:
            gen_out, ref_out, cover_out = (gen_low, ref_low, ref_hits)
        else:
            gen_out = jnp.minimum(gen_out, gen_low)
            ref_out = jnp.minimum(ref_out, ref_low)
            cover_out = cover_out + ref_hits
    gen_best = gen_out.reshape(GEN_FRAMES)
    ref_best = ref_out.reshape(REF_FRAMES)
    ref_cover = (cover_out / (STEPS * FRAMES)).reshape(REF_FRAMES)
    return (gen_best, ref_best, ref_cover)
```

```python
import functools

import jax
import jax.numpy as jnp
from jax import lax
from jax.experimental import pallas as pl
from jax.experimental.pallas import tpu as pltpu
from jax.sharding import PartitionSpec as P

POLAR = 8
STEPS = 2
DEPTH = 256
LANES = 128

soft_width = 0.25
floor_term = 0.01

THIRD = (
    0.8660254163908417, 0.16666504306323746, -0.048077350345029135, 0.024392383831939313,
    -0.014289564826206913, 0.007664301754289227, -0.002922830501063345, 0.0005426077123047435,
)


def split3(x):
    one = x.astype(jnp.bfloat16).astype(jnp.float32)
    rest = x - one
    two = rest.astype(jnp.bfloat16).astype(jnp.float32)
    return (one, two, rest - two)


def align_of(h):
    h00, h01, h02, h10, h11, h12, h20, h21, h22 = h
    s00 = h00 * h00 + h10 * h10 + h20 * h20
    s11 = h01 * h01 + h11 * h11 + h21 * h21
    s22 = h02 * h02 + h12 * h12 + h22 * h22
    s01 = h00 * h01 + h10 * h11 + h20 * h21
    s02 = h00 * h02 + h10 * h12 + h20 * h22
    s12 = h01 * h02 + h11 * h12 + h21 * h22
    det = (
        h00 * (h11 * h22 - h12 * h21)
        - h01 * (h10 * h22 - h12 * h20)
        + h02 * (h10 * h21 - h11 * h20)
    )
    trace = s00 + s11 + s22
    minors = (s00 * s11 - s01 * s01) + (s00 * s22 - s02 * s02) + (s11 * s22 - s12 * s12)
    size = trace + 1.0
    inverse = lax.rsqrt(size)
    inv2 = inverse * inverse
    third = trace * inv2 * (1.0 / 3.0)
    c2 = minors * (inv2 * inv2)
    det_n = det * (inv2 * inverse)
    third2 = third * third
    p2 = jnp.maximum(third2 - c2 * (1.0 / 3.0), 1e-12)
    half = third * (third2 - 0.5 * c2) + 0.5 * (det_n * det_n)
    ip = lax.rsqrt(p2)
    p = p2 * ip
    ratio = half * (ip * ip * ip)
    r = jnp.minimum(jnp.abs(ratio), 1.0)
    c = THIRD[-1] * r + THIRD[-2]
    for k in THIRD[-3::-1]:
        c = c * r + k
    rest = jnp.maximum(1.0 - c * c, 1e-14)
    wide = (p * 0.8660254037844386) * (rest * lax.rsqrt(rest))
    signed = jnp.where(half < 0.0, -p, p)
    pc = signed * c
    base = third * 0.5 - 0.5 * pc
    roots = (third * 0.5 + pc, base + wide, base - wide)
    total = None
    for root in roots:
        root = jnp.maximum(root, 1e-20)
        start = root * lax.rsqrt(root)
        v = start * (1.5 - root)
        for _ in range(POLAR - 1):
            v = v * (1.5 - v * v)
        total = start * v if total is None else total + start * v
    return (size * inverse) * total


def kernel(atoms, frames, chunk, rows, thr_ref, gen_ref, ref_ref, gmin_ref, rmin_ref, rsum_ref,
           ref_t, gen_b, h, rnb, gnb, rmin, rsum, gmin):
    scale = 1.0 / atoms

    def load(source, columns):
        parts = []
        sq = None
        for a in range(3):
            x = source[a, :, columns].astype(jnp.float32)
            total = jnp.sum(x, axis=0, keepdims=True)
            d = x - total * scale
            q = jnp.sum(d * d, axis=0, keepdims=True)
            sq = q if sq is None else sq + q
            parts.append((x, total))
        return parts, sq * scale

    def rows_of(values, columns):
        zero = jnp.zeros((DEPTH - atoms - 16, columns), jnp.float32)
        pick = lax.broadcasted_iota(jnp.int32, (16, columns), 0)
        extra = jnp.zeros((16, columns), jnp.float32)
        for k, value in enumerate(values):
            extra = jnp.where(pick == k, value, extra)
        return extra, zero

    for start in range(0, frames, 256):
        columns = slice(start, start + 256)
        parts, sq = load(ref_ref, columns)
        rnb[columns, :] = jnp.broadcast_to(sq + floor_term, (LANES, 256)).T
        for a, (x, total) in enumerate(parts):
            s = split3(-total)
            extra, zero = rows_of([s[k % 3] for k in range(9)], 256)
            ref_t[a, columns, :] = jnp.concatenate([x, extra, zero], axis=0).T.astype(jnp.bfloat16)
    rmin[...] = jnp.full(rmin.shape, jnp.inf, jnp.float32)
    rsum[...] = jnp.zeros(rsum.shape, jnp.float32)
    limit = thr_ref[0] * (1.4426950408889634 / soft_width)

    for start in range(0, frames, chunk):
        columns = slice(start, start + chunk)
        parts, sq = load(gen_ref, columns)
        gnb[...] = jnp.broadcast_to(sq, (8, chunk))
        for a, (x, total) in enumerate(parts):
            m = split3(total * scale)
            extra, zero = rows_of([m[k // 3] for k in range(9)], chunk)
            gen_b[...] = jnp.concatenate([x, extra, zero], axis=0).astype(jnp.bfloat16)
            for b in range(3):
                h[3 * a + b] = jnp.dot(ref_t[b], gen_b[...], preferred_element_type=jnp.float32)
        gmin[...] = jnp.full(gmin.shape, jnp.inf, jnp.float32)

        def group(index, carry):
            at = pl.ds(pl.multiple_of(index * rows, rows), rows)
            align = align_of([h[k, at, :] for k in range(9)])
            rn = rnb[at, :]
            rn = jnp.concatenate([rn] * (chunk // LANES), axis=1)
            gn = jnp.concatenate([gnb[...]] * (rows // 8), axis=0)
            square = rn + gn - align * (4.0 * scale)
            rmsd = square * lax.rsqrt(square)
            power = jnp.minimum(rmsd * (1.4426950408889634 / soft_width) - limit, 120.0)
            weight = 1.0 / (1.0 + jnp.exp2(power))
            low, hits = rmsd[:, :LANES], weight[:, :LANES]
            for k in range(1, chunk // LANES):
                low = jnp.minimum(low, rmsd[:, k * LANES:(k + 1) * LANES])
                hits = hits + weight[:, k * LANES:(k + 1) * LANES]
            rmin[at, :] = jnp.minimum(rmin[at, :], low)
            rsum[at, :] = rsum[at, :] + hits
            best = rmsd[:8]
            for k in range(1, rows // 8):
                best = jnp.minimum(best, rmsd[8 * k:8 * k + 8])
            gmin[...] = jnp.minimum(gmin[...], best)
            return carry

        lax.fori_loop(0, frames // rows, group, 0)
        gmin_ref[:, columns] = jnp.min(gmin[...], axis=0, keepdims=True)

    rmin_ref[...] = jnp.min(rmin[...].T, axis=0, keepdims=True)
    rsum_ref[...] = jnp.sum(rsum[...].T, axis=0, keepdims=True)


def tile(gen, ref, threshold):
    _, atoms, frames = gen.shape
    chunk, rows = 256, 8
    row = jax.ShapeDtypeStruct((1, frames), jnp.float32)
    vmem = pl.BlockSpec(memory_space=pltpu.VMEM)
    out = pl.pallas_call(
        functools.partial(kernel, atoms, frames, chunk, rows),
        out_shape=(row, row, row),
        in_specs=[pl.BlockSpec(memory_space=pltpu.SMEM), vmem, vmem],
        out_specs=(vmem, vmem, vmem),
        scratch_shapes=[
            pltpu.VMEM((3, frames, DEPTH), jnp.bfloat16),
            pltpu.VMEM((DEPTH, chunk), jnp.bfloat16),
            pltpu.VMEM((9, frames, chunk), jnp.float32),
            pltpu.VMEM((frames, LANES), jnp.float32),
            pltpu.VMEM((8, chunk), jnp.float32),
            pltpu.VMEM((frames, LANES), jnp.float32),
            pltpu.VMEM((frames, LANES), jnp.float32),
            pltpu.VMEM((8, chunk), jnp.float32),
        ],
        compiler_params=pltpu.CompilerParams(vmem_limit_bytes=40 * 2**20),
        cost_estimate=pl.CostEstimate(flops=2 * 9 * atoms * frames * frames + 250 * frames * frames,
                                      bytes_accessed=12 * atoms * frames, transcendentals=0),
    )(threshold, gen, ref)
    return [x.reshape(frames) for x in out]


def on_device(gen_coords, ref_coords, threshold):
    height, width = lax.axis_size("row"), lax.axis_size("col")
    frames = gen_coords.shape[2]
    sources = []
    for step in range(STEPS):
        source = {}
        turn = step + step // width
        for i in range(height):
            for j in range(width):
                gen_row = (i + turn) % height
                source[i * width + j] = gen_row * width + (j - gen_row - step) % width
        sources.append(source)
    blocks = [
        lax.ppermute(gen_coords, ("row", "col"), [(s, d) for d, s in source.items()])
        for source in sources
    ]
    gen_best = ref_best = hits = None
    for source, block in zip(sources, blocks):
        g, r, w = tile(block, ref_coords, threshold)
        g = lax.ppermute(g, ("row", "col"), list(source.items()))
        gen_best = g if gen_best is None else jnp.minimum(gen_best, g)
        ref_best = r if ref_best is None else jnp.minimum(ref_best, r)
        hits = w if hits is None else hits + w
    return (gen_best, ref_best, hits / (STEPS * frames))


def solution(mesh):
    spread = ("grp", "row", "col")
    return jax.shard_map(
        on_device,
        mesh=mesh,
        in_specs=(P(None, None, spread), P(None, None, spread), P()),
        out_specs=(P(spread), P(spread), P(spread)),
        check_vma=False,
    )
```

```python
import functools

import jax
import jax.numpy as jnp
from jax import lax
from jax.experimental import pallas as pl
from jax.experimental.pallas import tpu as pltpu
from jax.sharding import PartitionSpec as P

POLAR = 8
STEPS = 2
DEPTH = 256
LANES = 128
CHUNK, ROWS = 256, 32

soft_width = 0.25
floor_term = 0.01

THIRD = (
    0.8660254163908417, 0.16666504306323746, -0.048077350345029135, 0.024392383831939313,
    -0.014289564826206913, 0.007664301754289227, -0.002922830501063345, 0.0005426077123047435,
)


def split3(x):
    one = x.astype(jnp.bfloat16).astype(jnp.float32)
    rest = x - one
    two = rest.astype(jnp.bfloat16).astype(jnp.float32)
    return (one, two, rest - two)


def align_of(h):
    h00, h01, h02, h10, h11, h12, h20, h21, h22 = h
    s00 = h00 * h00 + h10 * h10 + h20 * h20
    s11 = h01 * h01 + h11 * h11 + h21 * h21
    s22 = h02 * h02 + h12 * h12 + h22 * h22
    s01 = h00 * h01 + h10 * h11 + h20 * h21
    s02 = h00 * h02 + h10 * h12 + h20 * h22
    s12 = h01 * h02 + h11 * h12 + h21 * h22
    q02 = s02 * s02
    q12 = s12 * s12
    m01 = s00 * s11 - s01 * s01
    minors = m01 + (s00 * s22 - q02) + (s11 * s22 - q12)
    cross = s01 * s02
    det = s22 * m01 - s11 * q02 - s00 * q12 + (cross + cross) * s12
    trace = s00 + s11 + s22
    size = trace + 1.0
    inverse = lax.rsqrt(size)
    inv2 = inverse * inverse
    third = trace * (1.0 / 3.0)
    third2 = third * third
    p2 = jnp.maximum(third2 - minors * (1.0 / 3.0), 1e-24)
    half = third * (third2 - 0.5 * minors) + 0.5 * det
    ip = lax.rsqrt(p2)
    p = (p2 * ip) * inv2
    r = jnp.minimum(jnp.abs(half * (ip * ip * ip)), 1.0)
    c = THIRD[-1] * r + THIRD[-2]
    for k in THIRD[-3::-1]:
        c = c * r + k
    rest = jnp.maximum(1.0 - c * c, 1e-14)
    wide = (p * 0.8660254037844386) * (rest * lax.rsqrt(rest))
    pc = jnp.where(half < 0.0, -p, p) * c
    middle = third * (0.5 * inv2)
    base = middle - 0.5 * pc
    total = None
    for root in (middle + pc, base + wide, base - wide):
        root = jnp.maximum(root, 1e-20)
        start = root * lax.rsqrt(root)
        v = start * (1.5 - root)
        for _ in range(POLAR - 1):
            v = v * (1.5 - v * v)
        total = start * v if total is None else total + start * v
    return (size * inverse) * total


def near_first(height, width):
    table = []
    for i in range(height):
        first = i % width
        second = ((i + 1) % height + 1) % width
        table.append(int(min(first, width - first) > min(second, width - second)))
    return table


def kernel(height, width, atoms, frames, chunk, rows, thr_ref, gen_ref, ref_ref,
           gbest_ref, rbest_ref, cover_ref, recv, back, ref_t, gen_b, h, rnb, gnb, rmin, rsum, gmin,
           send_sem, recv_sem, bsend_sem, brecv_sem):
    scale = 1.0 / atoms
    unit = 0.25 * atoms
    pieces = frames // chunk
    grp, i, j = lax.axis_index("grp"), lax.axis_index("row"), lax.axis_index("col")
    table = near_first(height, width)

    def slot_of(row):
        slot = jnp.int32(0)
        for k, late in enumerate(table):
            if late:
                slot = slot + jnp.where(row == k, 1, 0)
        return slot

    up, down = lax.rem(i + height - 1, height), lax.rem(i + 1, height)
    wrap = width * (height // width + 2)
    a_to = (grp, i, lax.rem(j + i, width))
    b_to = (grp, up, lax.rem(j + i + 1, width))
    a_from = (grp, i, lax.rem(j + wrap - i, width))
    b_from = (grp, down, lax.rem(j + wrap - down - 1, width))
    at_home = lax.rem(i, width) == 0
    away = lax.rem(i, width) != 0
    a_here = slot_of(i)
    a_slot, b_slot = a_here, 1 - slot_of(up)

    barrier = pltpu.get_barrier_semaphore()
    for other in (b_to, b_from):
        pl.semaphore_signal(barrier, inc=1, device_id=other, device_id_type=pl.DeviceIdType.MESH)

    @pl.when(away)
    def _():
        for other in (a_to, a_from):
            pl.semaphore_signal(barrier, inc=1, device_id=other, device_id_type=pl.DeviceIdType.MESH)

    pl.semaphore_wait(barrier, jnp.where(away, 4, 2))

    def remote(which, k):
        to, slot = ((a_to, a_slot), (b_to, b_slot))[which]
        columns = pl.ds(k * chunk, chunk)
        return pltpu.make_async_remote_copy(
            src_ref=gen_ref.at[:, :, columns], dst_ref=recv.at[slot, :, :, columns],
            send_sem=send_sem.at[which, k], recv_sem=recv_sem.at[slot, k],
            device_id=to, device_id_type=pl.DeviceIdType.MESH)

    def local(k):
        columns = pl.ds(k * chunk, chunk)
        return pltpu.make_async_copy(gen_ref.at[:, :, columns], recv.at[a_slot, :, :, columns],
                                     recv_sem.at[a_slot, k])

    def send(phase):
        @pl.when(jnp.logical_and(a_slot == phase, away))
        def _():
            for k in range(pieces):
                remote(0, k).start()

        @pl.when(jnp.logical_and(a_slot == phase, at_home))
        def _():
            for k in range(pieces):
                local(k).start()

        @pl.when(b_slot == phase)
        def _():
            for k in range(pieces):
                remote(1, k).start()

    send(0)

    def load(x_ref, columns):
        parts = []
        sq = None
        for a in range(3):
            x = x_ref[a, :, columns].astype(jnp.float32)
            total = jnp.sum(x, axis=0, keepdims=True)
            d = x - total * scale
            q = jnp.sum(d * d, axis=0, keepdims=True)
            sq = q if sq is None else sq + q
            parts.append((x, total))
        return parts, sq * (scale * unit)

    def deep(x, values, columns):
        pick = lax.broadcasted_iota(jnp.int32, (16, columns), 0)
        extra = jnp.zeros((16, columns), jnp.float32)
        for k, value in enumerate(values):
            extra = jnp.where(pick == k, value, extra)
        zero = jnp.zeros((DEPTH - atoms - 16, columns), jnp.float32)
        return jnp.concatenate([x, extra, zero], axis=0)

    def prepare(index, carry):
        columns = pl.ds(pl.multiple_of(index * chunk, chunk), chunk)
        parts, sq = load(ref_ref, columns)
        rnb[columns, :] = jnp.broadcast_to(sq + floor_term * unit, (LANES, chunk)).T
        for a, (x, total) in enumerate(parts):
            s = split3(-total)
            ref_t[a, columns, :] = deep(x, [s[k % 3] for k in range(9)], chunk).T.astype(jnp.bfloat16)
        return carry

    lax.fori_loop(0, pieces, prepare, 0)
    rmin[...] = jnp.full(rmin.shape, jnp.inf, jnp.float32)
    rsum[...] = jnp.zeros(rsum.shape, jnp.float32)
    gmin[...] = jnp.full(gmin.shape, jnp.inf, jnp.float32)
    slope = 1.4426950408889634 / soft_width
    limit = thr_ref[0] * slope
    slope = slope * unit ** -0.5

    def piece(slot):
        def run(index, carry):
            columns = pl.ds(pl.multiple_of(index * chunk, chunk), chunk)
            parts, sq = load(recv.at[slot], columns)
            gnb[...] = jnp.broadcast_to(sq, (8, chunk))
            for a, (x, total) in enumerate(parts):
                m = split3(total * scale)
                gen_b[...] = deep(x, [m[k // 3] for k in range(9)], chunk).astype(jnp.bfloat16)
                for b in range(3):
                    h[3 * a + b] = jnp.dot(ref_t[b], gen_b[...], preferred_element_type=jnp.float32)

            def group(step, carry):
                at = pl.ds(pl.multiple_of(step * rows, rows), rows)
                align = align_of([h[k, at, :] for k in range(9)])
                rn = jnp.concatenate([rnb[at, :]] * (chunk // LANES), axis=1)
                gn = jnp.concatenate([gnb[...]] * (rows // 8), axis=0)
                square = rn + gn - align
                rmsd = square * lax.rsqrt(square)
                power = jnp.minimum(rmsd * slope - limit, 120.0)
                below = 1.0 + jnp.exp2(power)
                weight = pl.reciprocal(below, approx=True)
                weight = weight * (2.0 - below * weight)
                low, hits = rmsd[:, :LANES], weight[:, :LANES]
                for k in range(1, chunk // LANES):
                    low = jnp.minimum(low, rmsd[:, k * LANES:(k + 1) * LANES])
                    hits = hits + weight[:, k * LANES:(k + 1) * LANES]
                rmin[at, :] = jnp.minimum(rmin[at, :], low)
                rsum[at, :] = rsum[at, :] + hits
                best = rmsd[:8]
                for k in range(1, rows // 8):
                    best = jnp.minimum(best, rmsd[8 * k:8 * k + 8])
                gmin[slot, :, columns] = jnp.minimum(gmin[slot, :, columns], best)
                return carry

            lax.fori_loop(0, frames // rows, group, 0)
            return carry
        return run

    def arrived(slot, k):
        target = recv.at[slot, :, :, pl.ds(k * chunk, chunk)]
        pltpu.make_async_copy(target, target, recv_sem.at[slot, k]).wait()

    def give_back(slot, which):
        return pltpu.make_async_remote_copy(
            src_ref=gmin.at[slot], dst_ref=back.at[which],
            send_sem=bsend_sem.at[slot], recv_sem=brecv_sem.at[which],
            device_id=(a_from, b_from)[which], device_id_type=pl.DeviceIdType.MESH)

    for slot in range(2):
        for k in range(pieces):
            arrived(slot, k)
            if slot == 0 and k == 0:
                send(1)
            piece(slot)(k, 0)
        here = a_here == slot

        @pl.when(jnp.logical_and(here, away))
        def _():
            give_back(slot, 0).start()

        @pl.when(jnp.logical_and(here, at_home))
        def _():
            pltpu.make_async_copy(gmin.at[slot], back.at[0], brecv_sem.at[0]).start()

        @pl.when(a_here != slot)
        def _():
            give_back(slot, 1).start()

    size = unit ** -0.5
    rbest_ref[...] = jnp.min(rmin[...].T, axis=0, keepdims=True) * size
    cover_ref[...] = jnp.sum(rsum[...].T, axis=0, keepdims=True) * (1.0 / (STEPS * frames))

    for which in range(2):
        pltpu.make_async_copy(back.at[which], back.at[which], brecv_sem.at[which]).wait()
    gbest_ref[...] = jnp.min(jnp.minimum(back[0], back[1]), axis=0, keepdims=True) * size

    @pl.when(away)
    def _():
        for k in range(pieces):
            remote(0, k).wait_send()

    for k in range(pieces):
        remote(1, k).wait_send()
    for slot in range(2):
        @pl.when(jnp.logical_or(away, a_here != slot))
        def _():
            give_back(slot, 0).wait_send()


def on_device(gen_coords, ref_coords, threshold):
    height, width = lax.axis_size("row"), lax.axis_size("col")
    _, atoms, frames = gen_coords.shape
    chunk, rows = min(CHUNK, frames), ROWS
    row = jax.ShapeDtypeStruct((1, frames), jnp.float32)
    vmem = pl.BlockSpec(memory_space=pltpu.VMEM)
    pieces = frames // chunk
    out = pl.pallas_call(
        functools.partial(kernel, height, width, atoms, frames, chunk, rows),
        out_shape=(row, row, row),
        in_specs=[pl.BlockSpec(memory_space=pltpu.SMEM), pl.BlockSpec(memory_space=pl.ANY), vmem],
        out_specs=(vmem, vmem, vmem),
        scratch_shapes=[
            pltpu.VMEM((2, 3, atoms, frames), jnp.bfloat16),
            pltpu.VMEM((2, 8, frames), jnp.float32),
            pltpu.VMEM((3, frames, DEPTH), jnp.bfloat16),
            pltpu.VMEM((DEPTH, chunk), jnp.bfloat16),
            pltpu.VMEM((9, frames, chunk), jnp.float32),
            pltpu.VMEM((frames, LANES), jnp.float32),
            pltpu.VMEM((8, chunk), jnp.float32),
            pltpu.VMEM((frames, LANES), jnp.float32),
            pltpu.VMEM((frames, LANES), jnp.float32),
            pltpu.VMEM((2, 8, frames), jnp.float32),
            pltpu.SemaphoreType.DMA((2, pieces)),
            pltpu.SemaphoreType.DMA((2, pieces)),
            pltpu.SemaphoreType.DMA((2,)),
            pltpu.SemaphoreType.DMA((2,)),
        ],
        compiler_params=pltpu.CompilerParams(
            vmem_limit_bytes=48 * 2**20, collective_id=0, has_side_effects=True),
    )(threshold, gen_coords, ref_coords)
    return tuple(x.reshape(frames) for x in out)


def solution(mesh):
    spread = ("grp", "row", "col")
    return jax.shard_map(
        on_device,
        mesh=mesh,
        in_specs=(P(None, None, spread), P(None, None, spread), P()),
        out_specs=(P(spread), P(spread), P(spread)),
        check_vma=False,
    )
```

```python
import functools

import jax
import jax.numpy as jnp
from jax import lax
from jax.experimental import pallas as pl
from jax.experimental.pallas import tpu as pltpu
from jax.sharding import PartitionSpec as P

POLAR = 8
STEPS = 2
DEPTH = 256
LANES = 128
CHUNK, ROWS = 256, 64

soft_width = 0.25
floor_term = 0.01

THIRD = (
    0.8660254163908417, 0.16666504306323746, -0.048077350345029135, 0.024392383831939313,
    -0.014289564826206913, 0.007664301754289227, -0.002922830501063345, 0.0005426077123047435,
)


def split3(x):
    one = x.astype(jnp.bfloat16).astype(jnp.float32)
    rest = x - one
    two = rest.astype(jnp.bfloat16).astype(jnp.float32)
    return (one, two, rest - two)


def align_of(h):
    h00, h01, h02, h10, h11, h12, h20, h21, h22 = h
    s00 = h00 * h00 + h10 * h10 + h20 * h20
    s11 = h01 * h01 + h11 * h11 + h21 * h21
    s22 = h02 * h02 + h12 * h12 + h22 * h22
    s01 = h00 * h01 + h10 * h11 + h20 * h21
    s02 = h00 * h02 + h10 * h12 + h20 * h22
    s12 = h01 * h02 + h11 * h12 + h21 * h22
    q02 = s02 * s02
    q12 = s12 * s12
    m01 = s00 * s11 - s01 * s01
    minors = m01 + (s00 * s22 - q02) + (s11 * s22 - q12)
    cross = s01 * s02
    det = s22 * m01 - s11 * q02 - s00 * q12 + (cross + cross) * s12
    trace = s00 + s11 + s22
    size = trace + 1.0
    inverse = lax.rsqrt(size)
    inv2 = inverse * inverse
    third = trace * (1.0 / 3.0)
    third2 = third * third
    p2 = jnp.maximum(third2 - minors * (1.0 / 3.0), 1e-24)
    half = third * (third2 - 0.5 * minors) + 0.5 * det
    ip = lax.rsqrt(p2)
    p = (p2 * ip) * inv2
    r = jnp.minimum(jnp.abs(half * (ip * ip * ip)), 1.0)
    c = THIRD[-1] * r + THIRD[-2]
    for k in THIRD[-3::-1]:
        c = c * r + k
    rest = jnp.maximum(1.0 - c * c, 1e-14)
    wide = (p * 0.8660254037844386) * (rest * lax.rsqrt(rest))
    pc = jnp.where(half < 0.0, -p, p) * c
    middle = third * (0.5 * inv2)
    base = middle - 0.5 * pc
    total = None
    for root in (middle + pc, base + wide, base - wide):
        root = jnp.maximum(root, 1e-20)
        start = root * lax.rsqrt(root)
        v = start * (1.5 - root)
        for _ in range(POLAR - 1):
            v = v * (1.5 - v * v)
        total = start * v if total is None else total + start * v
    return (size * inverse) * total


def near_first(height, width):
    table = []
    for i in range(height):
        first = i % width
        second = ((i + 1) % height + 1) % width
        table.append(int(min(first, width - first) > min(second, width - second)))
    return table


def handed_on(height, width):
    late = near_first(height, width)
    table = []
    for i in range(height):
        direct = (i + 1) % width
        near = min(direct, width - direct) <= 1
        table.append(int(i % width != 0 and not late[i] and late[i - 1] == 0 and not near))
    return table


def kernel(height, width, atoms, frames, chunk, rows, thr_ref, gen_ref, ref_hbm,
           gbest_ref, rbest_ref, cover_ref, ref_ref, recv, back, ref_t, gen_b, h, rnb, gnb, rmin, rsum, gmin,
           send_sem, recv_sem, bsend_sem, brecv_sem, ref_sem):
    fetch = pltpu.make_async_copy(ref_hbm, ref_ref, ref_sem)
    fetch.start()
    scale = 1.0 / atoms
    unit = 0.25 * atoms
    pieces = frames // chunk
    grp, i, j = lax.axis_index("grp"), lax.axis_index("row"), lax.axis_index("col")
    table = near_first(height, width)

    def entry(values, row):
        found = jnp.int32(0)
        for k, value in enumerate(values):
            if value:
                found = found + jnp.where(row == k, 1, 0)
        return found

    def slot_of(row):
        return entry(table, row)

    up, down = lax.rem(i + height - 1, height), lax.rem(i + 1, height)
    wrap = width * (height // width + 2)
    a_to = (grp, i, lax.rem(j + i, width))
    b_to = (grp, up, lax.rem(j + i + 1, width))
    a_from = (grp, i, lax.rem(j + wrap - i, width))
    b_from = (grp, down, lax.rem(j + wrap - down - 1, width))
    at_home = lax.rem(i, width) == 0
    away = lax.rem(i, width) != 0
    a_here = slot_of(i)
    a_slot, b_slot = a_here, 1 - slot_of(up)
    passing = entry(handed_on(height, width), i) == 1
    keeping = entry(handed_on(height, width), i) == 0
    next_to = (grp, up, lax.rem(j + 1, width))
    next_from = (grp, down, lax.rem(j + width - 1, width))
    sending = entry(handed_on(height, width), down) == 1

    barrier = pltpu.get_barrier_semaphore()
    for other in (b_to, b_from):
        pl.semaphore_signal(barrier, inc=1, device_id=other, device_id_type=pl.DeviceIdType.MESH)

    @pl.when(away)
    def _():
        for other in (a_to, a_from):
            pl.semaphore_signal(barrier, inc=1, device_id=other, device_id_type=pl.DeviceIdType.MESH)

    @pl.when(passing)
    def _():
        pl.semaphore_signal(barrier, inc=1, device_id=next_to, device_id_type=pl.DeviceIdType.MESH)

    @pl.when(sending)
    def _():
        pl.semaphore_signal(barrier, inc=1, device_id=next_from, device_id_type=pl.DeviceIdType.MESH)

    pl.semaphore_wait(
        barrier,
        2 + jnp.where(away, 2, 0) + jnp.where(passing, 1, 0) + jnp.where(sending, 1, 0))

    def remote(which, k):
        to, slot = ((a_to, a_slot), (b_to, b_slot))[which]
        columns = pl.ds(k * chunk, chunk)
        return pltpu.make_async_remote_copy(
            src_ref=gen_ref.at[:, :, columns], dst_ref=recv.at[slot, :, :, columns],
            send_sem=send_sem.at[which, k], recv_sem=recv_sem.at[slot, k],
            device_id=to, device_id_type=pl.DeviceIdType.MESH)

    def onward(k):
        columns = pl.ds(k * chunk, chunk)
        return pltpu.make_async_remote_copy(
            src_ref=recv.at[0, :, :, columns], dst_ref=recv.at[1, :, :, columns],
            send_sem=send_sem.at[1, k], recv_sem=recv_sem.at[1, k],
            device_id=next_to, device_id_type=pl.DeviceIdType.MESH)

    def local(k):
        columns = pl.ds(k * chunk, chunk)
        return pltpu.make_async_copy(gen_ref.at[:, :, columns], recv.at[a_slot, :, :, columns],
                                     recv_sem.at[a_slot, k])

    def send(phase):
        @pl.when(jnp.logical_and(a_slot == phase, away))
        def _():
            for k in range(pieces):
                remote(0, k).start()

        @pl.when(jnp.logical_and(a_slot == phase, at_home))
        def _():
            for k in range(pieces):
                local(k).start()

        @pl.when(jnp.logical_and(b_slot == phase, keeping))
        def _():
            for k in range(pieces):
                remote(1, k).start()

    send(0)

    def load(x_ref, columns):
        parts = []
        sq = None
        for a in range(3):
            x = x_ref[a, :, columns].astype(jnp.float32)
            total = jnp.sum(x, axis=0, keepdims=True)
            d = x - total * scale
            q = jnp.sum(d * d, axis=0, keepdims=True)
            sq = q if sq is None else sq + q
            parts.append((x, total))
        return parts, sq * (scale * unit)

    def deep(x, values, columns):
        pick = lax.broadcasted_iota(jnp.int32, (16, columns), 0)
        extra = jnp.zeros((16, columns), jnp.float32)
        for k, value in enumerate(values):
            extra = jnp.where(pick == k, value, extra)
        zero = jnp.zeros((DEPTH - atoms - 16, columns), jnp.float32)
        return jnp.concatenate([x, extra, zero], axis=0)

    def prepare(index, carry):
        columns = pl.ds(pl.multiple_of(index * chunk, chunk), chunk)
        parts, sq = load(ref_ref, columns)
        rnb[columns, :] = jnp.broadcast_to(sq + floor_term * unit, (LANES, chunk)).T
        for a, (x, total) in enumerate(parts):
            s = split3(-total)
            ref_t[a, columns, :] = deep(x, [s[k % 3] for k in range(9)], chunk).T.astype(jnp.bfloat16)
        return carry

    fetch.wait()
    lax.fori_loop(0, pieces, prepare, 0)
    rmin[...] = jnp.full(rmin.shape, jnp.inf, jnp.float32)
    rsum[...] = jnp.zeros(rsum.shape, jnp.float32)
    gmin[...] = jnp.full(gmin.shape, jnp.inf, jnp.float32)
    slope = 1.4426950408889634 / soft_width
    limit = thr_ref[0] * slope
    slope = slope * unit ** -0.5

    def piece(slot):
        def run(index, carry):
            columns = pl.ds(pl.multiple_of(index * chunk, chunk), chunk)
            parts, sq = load(recv.at[slot], columns)
            gnb[...] = jnp.broadcast_to(sq, (8, chunk))
            for a, (x, total) in enumerate(parts):
                m = split3(total * scale)
                gen_b[...] = deep(x, [m[k // 3] for k in range(9)], chunk).astype(jnp.bfloat16)
                for b in range(3):
                    h[3 * a + b] = jnp.dot(ref_t[b], gen_b[...], preferred_element_type=jnp.float32)

            def group(step, carry):
                at = pl.ds(pl.multiple_of(step * rows, rows), rows)
                align = align_of([h[k, at, :] for k in range(9)])
                rn = jnp.concatenate([rnb[at, :]] * (chunk // LANES), axis=1)
                gn = jnp.concatenate([gnb[...]] * (rows // 8), axis=0)
                square = rn + gn - align
                rmsd = square * lax.rsqrt(square)
                power = jnp.minimum(rmsd * slope - limit, 120.0)
                below = 1.0 + jnp.exp2(power)
                weight = pl.reciprocal(below, approx=True)
                weight = weight * (2.0 - below * weight)
                low, hits = rmsd[:, :LANES], weight[:, :LANES]
                for k in range(1, chunk // LANES):
                    low = jnp.minimum(low, rmsd[:, k * LANES:(k + 1) * LANES])
                    hits = hits + weight[:, k * LANES:(k + 1) * LANES]
                rmin[at, :] = jnp.minimum(rmin[at, :], low)
                rsum[at, :] = rsum[at, :] + hits
                best = rmsd[:8]
                for k in range(1, rows // 8):
                    best = jnp.minimum(best, rmsd[8 * k:8 * k + 8])
                gmin[slot, :, columns] = jnp.minimum(gmin[slot, :, columns], best)
                return carry

            lax.fori_loop(0, frames // rows, group, 0)
            return carry
        return run

    def arrived(slot, k):
        target = recv.at[slot, :, :, pl.ds(k * chunk, chunk)]
        pltpu.make_async_copy(target, target, recv_sem.at[slot, k]).wait()

    def give_back(slot, which):
        return pltpu.make_async_remote_copy(
            src_ref=gmin.at[slot], dst_ref=back.at[which],
            send_sem=bsend_sem.at[slot], recv_sem=brecv_sem.at[which],
            device_id=(a_from, b_from)[which], device_id_type=pl.DeviceIdType.MESH)

    for slot in range(2):
        for k in range(pieces):
            arrived(slot, k)
            if slot == 0 and k == 0:
                send(1)
            if slot == 0:
                @pl.when(passing)
                def _():
                    onward(k).start()

            piece(slot)(k, 0)
        here = a_here == slot

        @pl.when(jnp.logical_and(here, away))
        def _():
            give_back(slot, 0).start()

        @pl.when(jnp.logical_and(here, at_home))
        def _():
            pltpu.make_async_copy(gmin.at[slot], back.at[0], brecv_sem.at[0]).start()

        @pl.when(a_here != slot)
        def _():
            give_back(slot, 1).start()

    size = unit ** -0.5
    rbest_ref[...] = jnp.min(rmin[...].T, axis=0, keepdims=True) * size
    cover_ref[...] = jnp.sum(rsum[...].T, axis=0, keepdims=True) * (1.0 / (STEPS * frames))

    for which in range(2):
        pltpu.make_async_copy(back.at[which], back.at[which], brecv_sem.at[which]).wait()
    gbest_ref[...] = jnp.min(jnp.minimum(back[0], back[1]), axis=0, keepdims=True) * size

    @pl.when(away)
    def _():
        for k in range(pieces):
            remote(0, k).wait_send()

    for k in range(pieces):
        remote(1, k).wait_send()
    for slot in range(2):
        @pl.when(jnp.logical_or(away, a_here != slot))
        def _():
            give_back(slot, 0).wait_send()


def on_device(gen_coords, ref_coords, threshold):
    height, width = lax.axis_size("row"), lax.axis_size("col")
    _, atoms, frames = gen_coords.shape
    chunk, rows = min(CHUNK, frames), ROWS
    row = jax.ShapeDtypeStruct((1, frames), jnp.float32)
    vmem = pl.BlockSpec(memory_space=pltpu.VMEM)
    pieces = frames // chunk
    out = pl.pallas_call(
        functools.partial(kernel, height, width, atoms, frames, chunk, rows),
        out_shape=(row, row, row),
        in_specs=[pl.BlockSpec(memory_space=pltpu.SMEM)] + [pl.BlockSpec(memory_space=pltpu.HBM)] * 2,
        out_specs=(vmem, vmem, vmem),
        scratch_shapes=[
            pltpu.VMEM((3, atoms, frames), jnp.bfloat16),
            pltpu.VMEM((2, 3, atoms, frames), jnp.bfloat16),
            pltpu.VMEM((2, 8, frames), jnp.float32),
            pltpu.VMEM((3, frames, DEPTH), jnp.bfloat16),
            pltpu.VMEM((DEPTH, chunk), jnp.bfloat16),
            pltpu.VMEM((9, frames, chunk), jnp.float32),
            pltpu.VMEM((frames, LANES), jnp.float32),
            pltpu.VMEM((8, chunk), jnp.float32),
            pltpu.VMEM((frames, LANES), jnp.float32),
            pltpu.VMEM((frames, LANES), jnp.float32),
            pltpu.VMEM((2, 8, frames), jnp.float32),
            pltpu.SemaphoreType.DMA((2, pieces)),
            pltpu.SemaphoreType.DMA((2, pieces)),
            pltpu.SemaphoreType.DMA((2,)),
            pltpu.SemaphoreType.DMA((2,)),
            pltpu.SemaphoreType.DMA,
        ],
        compiler_params=pltpu.CompilerParams(
            vmem_limit_bytes=48 * 2**20, collective_id=0, has_side_effects=True),
    )(threshold, gen_coords, ref_coords)
    return tuple(x.reshape(frames) for x in out)


def solution(mesh):
    spread = ("grp", "row", "col")
    return jax.shard_map(
        on_device,
        mesh=mesh,
        in_specs=(P(None, None, spread), P(None, None, spread), P()),
        out_specs=(P(spread), P(spread), P(spread)),
        check_vma=False,
    )
```

```python
import functools

import jax
import jax.numpy as jnp
from jax import lax
from jax.experimental import pallas as pl
from jax.experimental.pallas import tpu as pltpu
from jax.sharding import PartitionSpec as P

POLAR = 8
STEPS = 2
DEPTH = 256
LANES = 128
CHUNK, ROWS = 256, 64

soft_width = 0.25
floor_term = 0.01

THIRD = (
    0.8660254163908417, 0.16666504306323746, -0.048077350345029135, 0.024392383831939313,
    -0.014289564826206913, 0.007664301754289227, -0.002922830501063345, 0.0005426077123047435,
)


def split3(x):
    one = x.astype(jnp.bfloat16).astype(jnp.float32)
    rest = x - one
    two = rest.astype(jnp.bfloat16).astype(jnp.float32)
    return (one, two, rest - two)


def align_of(h):
    h00, h01, h02, h10, h11, h12, h20, h21, h22 = h
    s00 = h00 * h00 + h10 * h10 + h20 * h20
    s11 = h01 * h01 + h11 * h11 + h21 * h21
    s22 = h02 * h02 + h12 * h12 + h22 * h22
    s01 = h00 * h01 + h10 * h11 + h20 * h21
    s02 = h00 * h02 + h10 * h12 + h20 * h22
    s12 = h01 * h02 + h11 * h12 + h21 * h22
    q02 = s02 * s02
    q12 = s12 * s12
    m01 = s00 * s11 - s01 * s01
    minors = m01 + (s00 * s22 - q02) + (s11 * s22 - q12)
    cross = s01 * s02
    det = s22 * m01 - s11 * q02 - s00 * q12 + (cross + cross) * s12
    trace = s00 + s11 + s22
    size = trace + 1.0
    inverse = lax.rsqrt(size)
    inv2 = inverse * inverse
    third = trace * (1.0 / 3.0)
    third2 = third * third
    p2 = jnp.maximum(third2 - minors * (1.0 / 3.0), 1e-24)
    half = third * (third2 - 0.5 * minors) + 0.5 * det
    ip = lax.rsqrt(p2)
    p = (p2 * ip) * inv2
    r = jnp.minimum(jnp.abs(half * (ip * ip * ip)), 1.0)
    c = THIRD[-1] * r + THIRD[-2]
    for k in THIRD[-3::-1]:
        c = c * r + k
    rest = jnp.maximum(1.0 - c * c, 1e-14)
    wide = (p * 0.8660254037844386) * (rest * lax.rsqrt(rest))
    pc = jnp.where(half < 0.0, -p, p) * c
    middle = third * (0.5 * inv2)
    base = middle - 0.5 * pc
    total = None
    for root in (middle + pc, base + wide, base - wide):
        root = jnp.maximum(root, 1e-20)
        start = root * lax.rsqrt(root)
        v = start * (1.5 - root)
        for _ in range(POLAR - 1):
            v = v * (1.5 - v * v)
        total = start * v if total is None else total + start * v
    return (size * inverse) * total


def near_first(height, width):
    table = []
    for i in range(height):
        first = i % width
        second = ((i + 1) % height + 1) % width
        table.append(int(min(first, width - first) > min(second, width - second)))
    return table


def handed_on(height, width):
    late = near_first(height, width)
    table = []
    for i in range(height):
        direct = (i + 1) % width
        near = min(direct, width - direct) <= 1
        table.append(int(i % width != 0 and not late[i] and late[i - 1] == 0 and not near))
    return table


def kernel(height, width, atoms, frames, chunk, rows, thr_ref, gen_ref, ref_hbm,
           gbest_ref, rbest_ref, cover_ref, ref_ref, recv, back, ref_t, gen_b, h, rnb, gnb, rmin, rsum, gmin,
           send_sem, recv_sem, bsend_sem, brecv_sem, ref_sem):
    fetch = pltpu.make_async_copy(ref_hbm, ref_ref, ref_sem)
    fetch.start()
    scale = 1.0 / atoms
    unit = 0.25 * atoms
    pieces = frames // chunk
    grp, i, j = lax.axis_index("grp"), lax.axis_index("row"), lax.axis_index("col")
    table = near_first(height, width)

    def entry(values, row):
        found = jnp.int32(0)
        for k, value in enumerate(values):
            if value:
                found = found + jnp.where(row == k, 1, 0)
        return found

    def slot_of(row):
        return entry(table, row)

    up, down = lax.rem(i + height - 1, height), lax.rem(i + 1, height)
    wrap = width * (height // width + 2)
    a_to = (grp, i, lax.rem(j + i, width))
    b_to = (grp, up, lax.rem(j + i + 1, width))
    a_from = (grp, i, lax.rem(j + wrap - i, width))
    b_from = (grp, down, lax.rem(j + wrap - down - 1, width))
    at_home = lax.rem(i, width) == 0
    away = lax.rem(i, width) != 0
    a_here = slot_of(i)
    a_slot, b_slot = a_here, 1 - slot_of(up)
    passes = entry(handed_on(height, width), i)
    passing = jnp.logical_and(passes == 1, j != width - 1)
    keeping = jnp.logical_or(passes == 0, lax.rem(j + i, width) == width - 1)
    next_to = (grp, up, lax.rem(j + 1, width))
    next_from = (grp, down, lax.rem(j + width - 1, width))
    sending = jnp.logical_and(entry(handed_on(height, width), down) == 1, j != 0)

    barrier = pltpu.get_barrier_semaphore()
    for other in (b_to, b_from):
        pl.semaphore_signal(barrier, inc=1, device_id=other, device_id_type=pl.DeviceIdType.MESH)

    @pl.when(away)
    def _():
        for other in (a_to, a_from):
            pl.semaphore_signal(barrier, inc=1, device_id=other, device_id_type=pl.DeviceIdType.MESH)

    @pl.when(passing)
    def _():
        pl.semaphore_signal(barrier, inc=1, device_id=next_to, device_id_type=pl.DeviceIdType.MESH)

    @pl.when(sending)
    def _():
        pl.semaphore_signal(barrier, inc=1, device_id=next_from, device_id_type=pl.DeviceIdType.MESH)

    pl.semaphore_wait(
        barrier,
        2 + jnp.where(away, 2, 0) + jnp.where(passing, 1, 0) + jnp.where(sending, 1, 0))

    def remote(which, k):
        to, slot = ((a_to, a_slot), (b_to, b_slot))[which]
        columns = pl.ds(k * chunk, chunk)
        return pltpu.make_async_remote_copy(
            src_ref=gen_ref.at[:, :, columns], dst_ref=recv.at[slot, :, :, columns],
            send_sem=send_sem.at[which, k], recv_sem=recv_sem.at[slot, k],
            device_id=to, device_id_type=pl.DeviceIdType.MESH)

    def onward(k):
        columns = pl.ds(k * chunk, chunk)
        return pltpu.make_async_remote_copy(
            src_ref=recv.at[0, :, :, columns], dst_ref=recv.at[1, :, :, columns],
            send_sem=send_sem.at[2, k], recv_sem=recv_sem.at[1, k],
            device_id=next_to, device_id_type=pl.DeviceIdType.MESH)

    def local(k):
        columns = pl.ds(k * chunk, chunk)
        return pltpu.make_async_copy(gen_ref.at[:, :, columns], recv.at[a_slot, :, :, columns],
                                     recv_sem.at[a_slot, k])

    def send(phase):
        @pl.when(jnp.logical_and(a_slot == phase, away))
        def _():
            for k in range(pieces):
                remote(0, k).start()

        @pl.when(jnp.logical_and(a_slot == phase, at_home))
        def _():
            for k in range(pieces):
                local(k).start()

        @pl.when(jnp.logical_and(b_slot == phase, keeping))
        def _():
            for k in range(pieces):
                remote(1, k).start()

    send(0)

    def load(x_ref, columns):
        parts = []
        sq = None
        for a in range(3):
            x = x_ref[a, :, columns].astype(jnp.float32)
            total = jnp.sum(x, axis=0, keepdims=True)
            d = x - total * scale
            q = jnp.sum(d * d, axis=0, keepdims=True)
            sq = q if sq is None else sq + q
            parts.append((x, total))
        return parts, sq * (scale * unit)

    def deep(x, values, columns):
        pick = lax.broadcasted_iota(jnp.int32, (16, columns), 0)
        extra = jnp.zeros((16, columns), jnp.float32)
        for k, value in enumerate(values):
            extra = jnp.where(pick == k, value, extra)
        zero = jnp.zeros((DEPTH - atoms - 16, columns), jnp.float32)
        return jnp.concatenate([x, extra, zero], axis=0)

    def prepare(index, carry):
        columns = pl.ds(pl.multiple_of(index * chunk, chunk), chunk)
        parts, sq = load(ref_ref, columns)
        rnb[columns, :] = jnp.broadcast_to(sq + floor_term * unit, (LANES, chunk)).T
        for a, (x, total) in enumerate(parts):
            s = split3(-total)
            ref_t[a, columns, :] = deep(x, [s[k % 3] for k in range(9)], chunk).T.astype(jnp.bfloat16)
        return carry

    fetch.wait()
    lax.fori_loop(0, pieces, prepare, 0)
    rmin[...] = jnp.full(rmin.shape, jnp.inf, jnp.float32)
    rsum[...] = jnp.zeros(rsum.shape, jnp.float32)
    gmin[...] = jnp.full(gmin.shape, jnp.inf, jnp.float32)
    slope = 1.4426950408889634 / soft_width
    limit = thr_ref[0] * slope
    slope = slope * unit ** -0.5

    def piece(slot):
        def run(index, carry):
            columns = pl.ds(pl.multiple_of(index * chunk, chunk), chunk)
            parts, sq = load(recv.at[slot], columns)
            gnb[...] = jnp.broadcast_to(sq, (8, chunk))
            for a, (x, total) in enumerate(parts):
                m = split3(total * scale)
                gen_b[...] = deep(x, [m[k // 3] for k in range(9)], chunk).astype(jnp.bfloat16)
                for b in range(3):
                    h[3 * a + b] = jnp.dot(ref_t[b], gen_b[...], preferred_element_type=jnp.float32)

            def group(step, carry):
                at = pl.ds(pl.multiple_of(step * rows, rows), rows)
                align = align_of([h[k, at, :] for k in range(9)])
                rn = jnp.concatenate([rnb[at, :]] * (chunk // LANES), axis=1)
                gn = jnp.concatenate([gnb[...]] * (rows // 8), axis=0)
                square = rn + gn - align
                rmsd = square * lax.rsqrt(square)
                power = jnp.minimum(rmsd * slope - limit, 120.0)
                below = 1.0 + jnp.exp2(power)
                weight = pl.reciprocal(below, approx=True)
                weight = weight * (2.0 - below * weight)
                low, hits = rmsd[:, :LANES], weight[:, :LANES]
                for k in range(1, chunk // LANES):
                    low = jnp.minimum(low, rmsd[:, k * LANES:(k + 1) * LANES])
                    hits = hits + weight[:, k * LANES:(k + 1) * LANES]
                rmin[at, :] = jnp.minimum(rmin[at, :], low)
                rsum[at, :] = rsum[at, :] + hits
                best = rmsd[:8]
                for k in range(1, rows // 8):
                    best = jnp.minimum(best, rmsd[8 * k:8 * k + 8])
                gmin[slot, :, columns] = jnp.minimum(gmin[slot, :, columns], best)
                return carry

            lax.fori_loop(0, frames // rows, group, 0)
            return carry
        return run

    def arrived(slot, k):
        target = recv.at[slot, :, :, pl.ds(k * chunk, chunk)]
        pltpu.make_async_copy(target, target, recv_sem.at[slot, k]).wait()

    def give_back(slot, which):
        return pltpu.make_async_remote_copy(
            src_ref=gmin.at[slot], dst_ref=back.at[which],
            send_sem=bsend_sem.at[slot], recv_sem=brecv_sem.at[which],
            device_id=(a_from, b_from)[which], device_id_type=pl.DeviceIdType.MESH)

    for slot in range(2):
        for k in range(pieces):
            arrived(slot, k)
            if slot == 0 and k == 0:
                send(1)
            if slot == 0:
                @pl.when(passing)
                def _():
                    onward(k).start()

            piece(slot)(k, 0)
        here = a_here == slot

        @pl.when(jnp.logical_and(here, away))
        def _():
            give_back(slot, 0).start()

        @pl.when(jnp.logical_and(here, at_home))
        def _():
            pltpu.make_async_copy(gmin.at[slot], back.at[0], brecv_sem.at[0]).start()

        @pl.when(a_here != slot)
        def _():
            give_back(slot, 1).start()

    size = unit ** -0.5
    rbest_ref[...] = jnp.min(rmin[...].T, axis=0, keepdims=True) * size
    cover_ref[...] = jnp.sum(rsum[...].T, axis=0, keepdims=True) * (1.0 / (STEPS * frames))

    for which in range(2):
        pltpu.make_async_copy(back.at[which], back.at[which], brecv_sem.at[which]).wait()
    gbest_ref[...] = jnp.min(jnp.minimum(back[0], back[1]), axis=0, keepdims=True) * size

    @pl.when(away)
    def _():
        for k in range(pieces):
            remote(0, k).wait_send()

    @pl.when(keeping)
    def _():
        for k in range(pieces):
            remote(1, k).wait_send()

    @pl.when(passing)
    def _():
        for k in range(pieces):
            onward(k).wait_send()

    for slot in range(2):
        @pl.when(jnp.logical_or(away, a_here != slot))
        def _():
            give_back(slot, 0).wait_send()


def on_device(gen_coords, ref_coords, threshold):
    height, width = lax.axis_size("row"), lax.axis_size("col")
    _, atoms, frames = gen_coords.shape
    chunk, rows = min(CHUNK, frames), ROWS
    row = jax.ShapeDtypeStruct((1, frames), jnp.float32)
    vmem = pl.BlockSpec(memory_space=pltpu.VMEM)
    pieces = frames // chunk
    out = pl.pallas_call(
        functools.partial(kernel, height, width, atoms, frames, chunk, rows),
        out_shape=(row, row, row),
        in_specs=[pl.BlockSpec(memory_space=pltpu.SMEM)] + [pl.BlockSpec(memory_space=pltpu.HBM)] * 2,
        out_specs=(vmem, vmem, vmem),
        scratch_shapes=[
            pltpu.VMEM((3, atoms, frames), jnp.bfloat16),
            pltpu.VMEM((2, 3, atoms, frames), jnp.bfloat16),
            pltpu.VMEM((2, 8, frames), jnp.float32),
            pltpu.VMEM((3, frames, DEPTH), jnp.bfloat16),
            pltpu.VMEM((DEPTH, chunk), jnp.bfloat16),
            pltpu.VMEM((9, frames, chunk), jnp.float32),
            pltpu.VMEM((frames, LANES), jnp.float32),
            pltpu.VMEM((8, chunk), jnp.float32),
            pltpu.VMEM((frames, LANES), jnp.float32),
            pltpu.VMEM((frames, LANES), jnp.float32),
            pltpu.VMEM((2, 8, frames), jnp.float32),
            pltpu.SemaphoreType.DMA((3, pieces)),
            pltpu.SemaphoreType.DMA((2, pieces)),
            pltpu.SemaphoreType.DMA((2,)),
            pltpu.SemaphoreType.DMA((2,)),
            pltpu.SemaphoreType.DMA,
        ],
        compiler_params=pltpu.CompilerParams(
            vmem_limit_bytes=48 * 2**20, collective_id=0, has_side_effects=True),
    )(threshold, gen_coords, ref_coords)
    return tuple(x.reshape(frames) for x in out)


def solution(mesh):
    spread = ("grp", "row", "col")
    return jax.shard_map(
        on_device,
        mesh=mesh,
        in_specs=(P(None, None, spread), P(None, None, spread), P()),
        out_specs=(P(spread), P(spread), P(spread)),
        check_vma=False,
    )
```

```python
import functools

import jax
import jax.numpy as jnp
from jax import lax
from jax.experimental import pallas as pl
from jax.experimental.pallas import tpu as pltpu
from jax.sharding import PartitionSpec as P

POLAR = 8
STEPS = 2
DEPTH = 256
LANES = 128
CHUNK, ROWS = 256, 64

soft_width = 0.25
floor_term = 0.01

THIRD = (
    0.8660254163908417, 0.16666504306323746, -0.048077350345029135, 0.024392383831939313,
    -0.014289564826206913, 0.007664301754289227, -0.002922830501063345, 0.0005426077123047435,
)


def split3(x):
    one = x.astype(jnp.bfloat16).astype(jnp.float32)
    rest = x - one
    two = rest.astype(jnp.bfloat16).astype(jnp.float32)
    return (one, two, rest - two)


def align_of(h):
    h00, h01, h02, h10, h11, h12, h20, h21, h22 = h
    s00 = h00 * h00 + h10 * h10 + h20 * h20
    s11 = h01 * h01 + h11 * h11 + h21 * h21
    s22 = h02 * h02 + h12 * h12 + h22 * h22
    s01 = h00 * h01 + h10 * h11 + h20 * h21
    s02 = h00 * h02 + h10 * h12 + h20 * h22
    s12 = h01 * h02 + h11 * h12 + h21 * h22
    q02 = s02 * s02
    q12 = s12 * s12
    m01 = s00 * s11 - s01 * s01
    minors = m01 + (s00 * s22 - q02) + (s11 * s22 - q12)
    cross = s01 * s02
    det = s22 * m01 - s11 * q02 - s00 * q12 + (cross + cross) * s12
    trace = s00 + s11 + s22
    size = trace + 1.0
    inverse = lax.rsqrt(size)
    inv2 = inverse * inverse
    third = trace * (1.0 / 3.0)
    third2 = third * third
    p2 = jnp.maximum(third2 - minors * (1.0 / 3.0), 1e-24)
    half = third * (third2 - 0.5 * minors) + 0.5 * det
    ip = lax.rsqrt(p2)
    p = (p2 * ip) * inv2
    r = jnp.minimum(jnp.abs(half * (ip * ip * ip)), 1.0)
    c = THIRD[-1] * r + THIRD[-2]
    for k in THIRD[-3::-1]:
        c = c * r + k
    rest = jnp.maximum(1.0 - c * c, 1e-14)
    wide = (p * 0.8660254037844386) * (rest * lax.rsqrt(rest))
    pc = jnp.where(half < 0.0, -p, p) * c
    middle = third * (0.5 * inv2)
    base = middle - 0.5 * pc
    total = None
    for root in (middle + pc, base + wide, base - wide):
        root = jnp.maximum(root, 1e-20)
        start = root * lax.rsqrt(root)
        v = start * (1.5 - root)
        for _ in range(POLAR - 1):
            v = v * (1.5 - v * v)
        total = start * v if total is None else total + start * v
    return (size * inverse) * total


def near_first(height, width):
    table = []
    for i in range(height):
        first = i % width
        second = ((i + 1) % height + 1) % width
        table.append(int(min(first, width - first) > min(second, width - second)))
    return table


def handed_on(height, width):
    late = near_first(height, width)
    table = []
    for i in range(height):
        direct = (i + 1) % width
        near = min(direct, width - direct) <= 1
        table.append(int(i % width != 0 and not late[i] and late[i - 1] == 0 and not near))
    return table


def kernel(height, width, atoms, frames, chunk, rows, thr_ref, gen_ref, ref_hbm,
           gbest_ref, rbest_ref, cover_ref, ref_ref, recv, back, ref_t, gen_b, h, rnb, gnb, rmin, rsum, gmin,
           send_sem, recv_sem, bsend_sem, brecv_sem, ref_sem):
    fetch = pltpu.make_async_copy(ref_hbm, ref_ref, ref_sem)
    fetch.start()
    scale = 1.0 / atoms
    unit = 0.25 * atoms
    pieces = frames // chunk
    grp, i, j = lax.axis_index("grp"), lax.axis_index("row"), lax.axis_index("col")
    table = near_first(height, width)

    def entry(values, row):
        found = jnp.int32(0)
        for k, value in enumerate(values):
            if value:
                found = found + jnp.where(row == k, 1, 0)
        return found

    def slot_of(row):
        return entry(table, row)

    up, down = lax.rem(i + height - 1, height), lax.rem(i + 1, height)
    wrap = width * (height // width + 2)
    a_to = (grp, i, lax.rem(j + i, width))
    b_to = (grp, up, lax.rem(j + i + 1, width))
    a_from = (grp, i, lax.rem(j + wrap - i, width))
    b_from = (grp, down, lax.rem(j + wrap - down - 1, width))
    at_home = lax.rem(i, width) == 0
    away = lax.rem(i, width) != 0
    a_here = slot_of(i)
    a_slot, b_slot = a_here, 1 - slot_of(up)
    passes = entry(handed_on(height, width), i)
    passing = jnp.logical_and(passes == 1, j != width - 1)
    keeping = jnp.logical_or(passes == 0, lax.rem(j + i, width) == width - 1)
    next_to = (grp, up, lax.rem(j + 1, width))
    next_from = (grp, down, lax.rem(j + width - 1, width))
    sending = jnp.logical_and(entry(handed_on(height, width), down) == 1, j != 0)

    barrier = pltpu.get_barrier_semaphore()
    for other in (b_to, b_from):
        pl.semaphore_signal(barrier, inc=1, device_id=other, device_id_type=pl.DeviceIdType.MESH)

    @pl.when(away)
    def _():
        for other in (a_to, a_from):
            pl.semaphore_signal(barrier, inc=1, device_id=other, device_id_type=pl.DeviceIdType.MESH)

    @pl.when(passing)
    def _():
        pl.semaphore_signal(barrier, inc=1, device_id=next_to, device_id_type=pl.DeviceIdType.MESH)

    @pl.when(sending)
    def _():
        pl.semaphore_signal(barrier, inc=1, device_id=next_from, device_id_type=pl.DeviceIdType.MESH)

    pl.semaphore_wait(
        barrier,
        2 + jnp.where(away, 2, 0) + jnp.where(passing, 1, 0) + jnp.where(sending, 1, 0))

    def remote(which, k):
        to, slot = ((a_to, a_slot), (b_to, b_slot))[which]
        columns = pl.ds(k * chunk, chunk)
        return pltpu.make_async_remote_copy(
            src_ref=gen_ref.at[:, :, columns], dst_ref=recv.at[slot, :, :, columns],
            send_sem=send_sem.at[which, k], recv_sem=recv_sem.at[slot, k],
            device_id=to, device_id_type=pl.DeviceIdType.MESH)

    def onward(k):
        columns = pl.ds(k * chunk, chunk)
        return pltpu.make_async_remote_copy(
            src_ref=recv.at[0, :, :, columns], dst_ref=recv.at[1, :, :, columns],
            send_sem=send_sem.at[2, k], recv_sem=recv_sem.at[1, k],
            device_id=next_to, device_id_type=pl.DeviceIdType.MESH)

    def local(k):
        columns = pl.ds(k * chunk, chunk)
        return pltpu.make_async_copy(gen_ref.at[:, :, columns], recv.at[a_slot, :, :, columns],
                                     recv_sem.at[a_slot, k])

    def send(phase):
        @pl.when(jnp.logical_and(a_slot == phase, away))
        def _():
            for k in range(pieces):
                remote(0, k).start()

        @pl.when(jnp.logical_and(a_slot == phase, at_home))
        def _():
            for k in range(pieces):
                local(k).start()

        @pl.when(jnp.logical_and(b_slot == phase, keeping))
        def _():
            for k in range(pieces):
                remote(1, k).start()

    send(0)

    def load(x_ref, columns):
        parts = []
        sq = None
        for a in range(3):
            x = x_ref[a, :, columns].astype(jnp.float32)
            total = jnp.sum(x, axis=0, keepdims=True)
            d = x - total * scale
            q = jnp.sum(d * d, axis=0, keepdims=True)
            sq = q if sq is None else sq + q
            parts.append((x, total))
        return parts, sq * (scale * unit)

    def deep(x, values, columns):
        pick = lax.broadcasted_iota(jnp.int32, (16, columns), 0)
        extra = jnp.zeros((16, columns), jnp.float32)
        for k, value in enumerate(values):
            extra = jnp.where(pick == k, value, extra)
        zero = jnp.zeros((DEPTH - atoms - 16, columns), jnp.float32)
        return jnp.concatenate([x, extra, zero], axis=0)

    def prepare(index, carry):
        columns = pl.ds(pl.multiple_of(index * chunk, chunk), chunk)
        parts, sq = load(ref_ref, columns)
        rnb[columns, :] = jnp.broadcast_to(sq + floor_term * unit, (LANES, chunk)).T
        for a, (x, total) in enumerate(parts):
            s = split3(-total)
            ref_t[a, columns, :] = deep(x, [s[k % 3] for k in range(9)], chunk).T.astype(jnp.bfloat16)
        return carry

    send(1)
    fetch.wait()
    lax.fori_loop(0, pieces, prepare, 0)
    rmin[...] = jnp.full(rmin.shape, jnp.inf, jnp.float32)
    rsum[...] = jnp.zeros(rsum.shape, jnp.float32)
    gmin[...] = jnp.full(gmin.shape, jnp.inf, jnp.float32)
    slope = 1.4426950408889634 / soft_width
    limit = thr_ref[0] * slope
    slope = slope * unit ** -0.5

    def piece(slot):
        def run(index, carry):
            columns = pl.ds(pl.multiple_of(index * chunk, chunk), chunk)
            parts, sq = load(recv.at[slot], columns)
            gnb[...] = jnp.broadcast_to(sq, (8, chunk))
            for a, (x, total) in enumerate(parts):
                m = split3(total * scale)
                gen_b[...] = deep(x, [m[k // 3] for k in range(9)], chunk).astype(jnp.bfloat16)
                for b in range(3):
                    h[3 * a + b] = jnp.dot(ref_t[b], gen_b[...], preferred_element_type=jnp.float32)

            def group(step, carry):
                at = pl.ds(pl.multiple_of(step * rows, rows), rows)
                align = align_of([h[k, at, :] for k in range(9)])
                rn = jnp.concatenate([rnb[at, :]] * (chunk // LANES), axis=1)
                gn = jnp.concatenate([gnb[...]] * (rows // 8), axis=0)
                square = rn + gn - align
                rmsd = square * lax.rsqrt(square)
                power = jnp.minimum(rmsd * slope - limit, 120.0)
                below = 1.0 + jnp.exp2(power)
                weight = pl.reciprocal(below, approx=True)
                weight = weight * (2.0 - below * weight)
                low, hits = rmsd[:, :LANES], weight[:, :LANES]
                for k in range(1, chunk // LANES):
                    low = jnp.minimum(low, rmsd[:, k * LANES:(k + 1) * LANES])
                    hits = hits + weight[:, k * LANES:(k + 1) * LANES]
                rmin[at, :] = jnp.minimum(rmin[at, :], low)
                rsum[at, :] = rsum[at, :] + hits
                best = rmsd[:8]
                for k in range(1, rows // 8):
                    best = jnp.minimum(best, rmsd[8 * k:8 * k + 8])
                gmin[slot, :, columns] = jnp.minimum(gmin[slot, :, columns], best)
                return carry

            lax.fori_loop(0, frames // rows, group, 0)
            return carry
        return run

    def arrived(slot, k):
        target = recv.at[slot, :, :, pl.ds(k * chunk, chunk)]
        pltpu.make_async_copy(target, target, recv_sem.at[slot, k]).wait()

    def give_back(slot, which):
        return pltpu.make_async_remote_copy(
            src_ref=gmin.at[slot], dst_ref=back.at[which],
            send_sem=bsend_sem.at[slot], recv_sem=brecv_sem.at[which],
            device_id=(a_from, b_from)[which], device_id_type=pl.DeviceIdType.MESH)

    for slot in range(2):
        for k in range(pieces):
            arrived(slot, k)
            if slot == 0:
                @pl.when(passing)
                def _():
                    onward(k).start()

            piece(slot)(k, 0)
        here = a_here == slot

        @pl.when(jnp.logical_and(here, away))
        def _():
            give_back(slot, 0).start()

        @pl.when(jnp.logical_and(here, at_home))
        def _():
            pltpu.make_async_copy(gmin.at[slot], back.at[0], brecv_sem.at[0]).start()

        @pl.when(a_here != slot)
        def _():
            give_back(slot, 1).start()

    size = unit ** -0.5
    rbest_ref[...] = jnp.min(rmin[...].T, axis=0, keepdims=True) * size
    cover_ref[...] = jnp.sum(rsum[...].T, axis=0, keepdims=True) * (1.0 / (STEPS * frames))

    for which in range(2):
        pltpu.make_async_copy(back.at[which], back.at[which], brecv_sem.at[which]).wait()
    gbest_ref[...] = jnp.min(jnp.minimum(back[0], back[1]), axis=0, keepdims=True) * size

    @pl.when(away)
    def _():
        for k in range(pieces):
            remote(0, k).wait_send()

    @pl.when(keeping)
    def _():
        for k in range(pieces):
            remote(1, k).wait_send()

    @pl.when(passing)
    def _():
        for k in range(pieces):
            onward(k).wait_send()

    for slot in range(2):
        @pl.when(jnp.logical_or(away, a_here != slot))
        def _():
            give_back(slot, 0).wait_send()


def on_device(gen_coords, ref_coords, threshold):
    height, width = lax.axis_size("row"), lax.axis_size("col")
    _, atoms, frames = gen_coords.shape
    chunk, rows = min(CHUNK, frames), ROWS
    row = jax.ShapeDtypeStruct((1, frames), jnp.float32)
    vmem = pl.BlockSpec(memory_space=pltpu.VMEM)
    pieces = frames // chunk
    out = pl.pallas_call(
        functools.partial(kernel, height, width, atoms, frames, chunk, rows),
        out_shape=(row, row, row),
        in_specs=[pl.BlockSpec(memory_space=pltpu.SMEM)] + [pl.BlockSpec(memory_space=pltpu.HBM)] * 2,
        out_specs=(vmem, vmem, vmem),
        scratch_shapes=[
            pltpu.VMEM((3, atoms, frames), jnp.bfloat16),
            pltpu.VMEM((2, 3, atoms, frames), jnp.bfloat16),
            pltpu.VMEM((2, 8, frames), jnp.float32),
            pltpu.VMEM((3, frames, DEPTH), jnp.bfloat16),
            pltpu.VMEM((DEPTH, chunk), jnp.bfloat16),
            pltpu.VMEM((9, frames, chunk), jnp.float32),
            pltpu.VMEM((frames, LANES), jnp.float32),
            pltpu.VMEM((8, chunk), jnp.float32),
            pltpu.VMEM((frames, LANES), jnp.float32),
            pltpu.VMEM((frames, LANES), jnp.float32),
            pltpu.VMEM((2, 8, frames), jnp.float32),
            pltpu.SemaphoreType.DMA((3, pieces)),
            pltpu.SemaphoreType.DMA((2, pieces)),
            pltpu.SemaphoreType.DMA((2,)),
            pltpu.SemaphoreType.DMA((2,)),
            pltpu.SemaphoreType.DMA,
        ],
        compiler_params=pltpu.CompilerParams(
            vmem_limit_bytes=48 * 2**20, collective_id=0, has_side_effects=True),
    )(threshold, gen_coords, ref_coords)
    return tuple(x.reshape(frames) for x in out)


def solution(mesh):
    spread = ("grp", "row", "col")
    return jax.shard_map(
        on_device,
        mesh=mesh,
        in_specs=(P(None, None, spread), P(None, None, spread), P()),
        out_specs=(P(spread), P(spread), P(spread)),
        check_vma=False,
    )
```
